32 devices in a mesh: row: 16 (over z, y, core), rep: 2 (over x).
Axes of the slice: x: 2, y: 2, z: 4, core: 2. Of those that a mesh axis runs over, the one named last changes fastest.
Arguments:
- features: bfloat16 [12288, 256], P('row'), may hold values from -7 to 7
- adjacency: bfloat16 [12288, 12288], P('row', 'rep'), may hold values from -0.078125 to 0.078125
- tile_live: int32 [16, 16], P('row', 'rep'), may hold values from 0 to 1, as said below
- w_self: bfloat16 [256, 256], replicated, may hold values from -1.25 to 1.25
- w_neigh: bfloat16 [256, 256], replicated, may hold values from -1.25 to 1.25
- bias_vector: float32 [256], replicated, may hold values from -3 to 3
- pos_pairs: int32 [16, 256, 3], P('row', 'rep'), may hold values from 0 to 640, as said below
- neg_pairs: int32 [16, 256, 3], P('row', 'rep'), may hold values from 0 to 640, as said below
Outputs:
- embedding: bfloat16 [12288, 256], P(('row', 'rep'))
- pos_loss: float32 [16, 256, 128], P('row', 'rep')
- neg_loss: float32 [16, 256, 128], P('row', 'rep')
The draws below stay inside these ranges and needn't reach their ends.
Inputs may be any that keep to these rules, and one draw needn't show every extreme that they name: `tile_live`: 1 marks a tile that counts (the adjacency holds nonzero values in every tile, live or not); every diagonal tile is live. `pos_pairs`: column 0 is below 6, column 1 below 8, column 2 at most 640, which is reached. `neg_pairs`: column 0 is below 6, column 1 below 8, column 2 at most 640, which is reached.
All inputs are finite; a program needn't handle non-finite values.
Results may differ from the reference program's by a relative error of at most 0.0037.
Values may be sent and summed in bfloat16 or wider, within the bound.
No kernel may reach another device: no remote copies, remote signals or barrier semaphores. Data moves between devices by JAX's collectives and lax.ppermute only.
A program may use at most 128 MiB of HBM per device.

```python
import math
import jax
import jax.numpy as jnp
from jax import lax

F = 256
BLOCK = 768
PAIRS = 128
PAIR_ROWS = 128
NODES = 12288
N_ROW = 16
N_REP = 2


def pair_table(key):
    first = jax.random.randint(jax.random.fold_in(key, 1), (N_ROW, N_REP * PAIRS), 0, BLOCK // PAIR_ROWS)
    second = jax.random.randint(jax.random.fold_in(key, 2), (N_ROW, N_REP * PAIRS), 0, N_ROW // N_REP)
    offsets = jax.random.randint(jax.random.fold_in(key, 3), (N_ROW, N_REP * PAIRS), 0, BLOCK - PAIR_ROWS + 1)
    offsets = offsets.at[0, 0].set(BLOCK - PAIR_ROWS)
    offsets = offsets.at[0, 1].set(0)
    return jnp.stack([first, second, offsets], axis=-1).astype(jnp.int32)


def signed_diagonal(key, noise, spread):
    signs = (jax.random.randint(jax.random.fold_in(key, 1), (F,), 0, 2) * 2 - 1).astype(jnp.float32)
    rows_idx = jnp.arange(F, dtype=jnp.int32)[:, None]
    cols_idx = jnp.arange(F, dtype=jnp.int32)[None, :]
    diagonal = jnp.where(rows_idx == cols_idx, signs[:, None], 0.0)
    return (diagonal + noise * (spread / jnp.sqrt(jnp.float32(F)))).astype(jnp.bfloat16)


def draw_features(key, part):
    key = jax.random.fold_in(key, 5)
    block_keys = jax.random.split(jax.random.fold_in(key, 1), N_ROW)
    ranks = jax.vmap(lambda one_key: jax.random.permutation(one_key, F))(block_keys)
    spread = jnp.exp(jnp.log(3.0) * (ranks.astype(jnp.float32) / (F - 1) - 0.5))
    row_scale = jnp.repeat(spread, BLOCK, axis=0, total_repeat_length=NODES)
    base = jnp.clip(jax.random.normal(jax.random.fold_in(key, 2), (NODES, F), jnp.float32), -4.0, 4.0)
    return (base * row_scale).astype(jnp.bfloat16)


def draw_w_self(key, part):
    key = jax.random.fold_in(key, 41)
    noise = jnp.clip(jax.random.normal(jax.random.fold_in(key, 2), (F, F), jnp.float32), -4.0, 4.0)
    return signed_diagonal(key, noise, 0.25)


def draw_w_neigh(key, part):
    key = jax.random.fold_in(key, 53)
    noise = jnp.clip(jax.random.normal(jax.random.fold_in(key, 2), (F, F), jnp.float32), -4.0, 4.0)
    return signed_diagonal(key, noise, 0.25)


def draw_tile_live(key, part):
    key = jax.random.fold_in(key, 11)
    rows_idx = jnp.arange(N_ROW, dtype=jnp.int32)[:, None]
    cols_idx = jnp.arange(N_ROW, dtype=jnp.int32)[None, :]
    distance = jnp.abs(rows_idx - cols_idx)
    distance = jnp.minimum(distance, N_ROW - distance)
    threshold = jnp.where(distance == 0, 100, jnp.where(distance <= 2, 60, 15))
    rolled = jax.random.randint(key, (N_ROW, N_ROW), 0, 100)
    return (rolled < threshold).astype(jnp.int32)


def draw_pos_pairs(key, part):
    key = jax.random.fold_in(key, 21)
    return pair_table(key)


def draw_neg_pairs(key, part):
    key = jax.random.fold_in(key, 37)
    return pair_table(key)


def levels(rng, dims, pieces, smallest, largest):
    level = 1.0
    for axis_at, blocks in pieces:
        heights = jax.random.uniform(jax.random.fold_in(jax.random.fold_in(rng, 6), axis_at), (blocks,), jnp.float32, smallest / len(pieces), largest / len(pieces))
        level = level * jnp.repeat(jnp.exp(heights), dims[axis_at] // blocks).reshape((-1,) + (1,) * (len(dims) - 1 - axis_at))
    return level


def bell_draw(own_key, extent, scale, bound, pieces=(), kind=jnp.bfloat16):
    array = jax.random.normal(own_key, extent, jnp.float32) * scale
    if len(pieces) > 0:
        array = levels(own_key, extent, pieces, -0.22, 0.18) * array
    return jnp.clip(array, min=-bound, max=bound).astype(kind)


def setup_inputs(seed: int = 0) -> dict:
    streams_of = jax.random.split(jax.random.key(seed), 9)
    features = draw_features(jax.random.fold_in(streams_of[8], 71), 0)
    adjacency = bell_draw(streams_of[1], (NODES, NODES), (8 * BLOCK) ** -0.5, 0.078125, ((0, 16), (1, 2)))
    tile_live = draw_tile_live(jax.random.fold_in(streams_of[8], 71), 0)
    w_self = draw_w_self(jax.random.fold_in(streams_of[8], 71), 0)
    w_neigh = draw_w_neigh(jax.random.fold_in(streams_of[8], 71), 0)
    bias_vector = bell_draw(streams_of[5], (F,), 0.5, 3.0, (), jnp.float32)
    pos_pairs = draw_pos_pairs(jax.random.fold_in(streams_of[8], 71), 0)
    neg_pairs = draw_neg_pairs(jax.random.fold_in(streams_of[8], 71), 0)
    return {"features": features, "adjacency": adjacency, "tile_live": tile_live, "w_self": w_self, "w_neigh": w_neigh, "bias_vector": bias_vector, "pos_pairs": pos_pairs, "neg_pairs": neg_pairs}


def reference(features, adjacency, tile_live, w_self, w_neigh, bias_vector, pos_pairs, neg_pairs):

    def aggregate(row_idx):
        tile_rows = lax.dynamic_slice_in_dim(adjacency, row_idx * BLOCK, BLOCK, 0)
        flags = lax.dynamic_index_in_dim(tile_live, row_idx, 0, keepdims=False)
        col_flags = jnp.repeat(flags, BLOCK).astype(adjacency.dtype)
        return jnp.dot(tile_rows * col_flags[None, :], features, preferred_element_type=jnp.float32)
    neighbour = lax.map(aggregate, jnp.arange(N_ROW, dtype=jnp.int32)).reshape(NODES, F)
    projected = jnp.dot(features, w_self, preferred_element_type=jnp.float32)
    projected = projected + jnp.dot(neighbour.astype(jnp.bfloat16), w_neigh, preferred_element_type=jnp.float32)
    projected = projected + bias_vector.astype(jnp.float32)
    scaled = projected * lax.rsqrt(lax.optimization_barrier(jnp.mean(projected * projected, axis=-1, keepdims=True)) + 1e-06)
    embedding = scaled.astype(jnp.bfloat16)
    blocked = embedding.reshape(N_ROW, BLOCK, F)
    zero_index = jnp.zeros((), jnp.int32)

    def losses_for(pairs, direction):

        def one_row(inputs):
            row_idx, row_pairs = inputs
            query_tiles = blocked[row_idx].reshape(BLOCK // PAIR_ROWS, PAIR_ROWS, F)
            queries = query_tiles[row_pairs[:, 0]]
            replica_idx = (jnp.arange(N_REP * PAIRS, dtype=jnp.int32) // PAIRS).astype(jnp.int32)
            key_block = (replica_idx * (N_ROW // N_REP) + row_pairs[:, 1]).astype(jnp.int32)

            def take_keys(block_id, offset):
                return lax.dynamic_slice(blocked, (block_id, offset, zero_index), (1, PAIR_ROWS, F))[0]
            key_rows = jax.vmap(take_keys)(key_block, row_pairs[:, 2].astype(jnp.int32))
            scores = jnp.einsum('pqf,pkf->pqk', queries.astype(jnp.float32), key_rows.astype(jnp.float32)) / math.sqrt(F)
            return lax.optimization_barrier(jnp.mean(jax.nn.softplus(direction * scores), axis=-1))
        return lax.map(one_row, (jnp.arange(N_ROW, dtype=jnp.int32), pairs))
    pos_loss = losses_for(pos_pairs, -1.0)
    neg_loss = losses_for(neg_pairs, 1.0)
    return (embedding, pos_loss, neg_loss)
```

```python
import functools
import math

import jax
import jax.numpy as jnp
from jax import lax
from jax.experimental import pallas as pl
from jax.experimental.pallas import tpu as pltpu
from jax.sharding import PartitionSpec as P

PAIR_ROWS = 128
EDGE = 8
UNROLL = 8
WIDE = 256


def permute(block, pairs, n_rep):
    return lax.ppermute(
        block, ("row", "rep"), [(a[0] * n_rep + a[1], b[0] * n_rep + b[1]) for a, b in pairs]
    )


def aggregate_kernel(rows_of, members, fetch, sections, has_tiles, has_previous, live_ref, *refs):
    n_pieces = sum(len(rows) for rows in rows_of)
    piece_refs, refs = refs[:n_pieces], refs[n_pieces:]
    previous_ref, refs = (refs[0], refs[1:]) if has_previous else (None, refs)
    if has_tiles:
        tile_refs, (out_ref,) = refs[: len(members)], refs[len(members) :]
    else:
        adjacency_ref, out_ref = refs[:2]
        fetch_refs, (tiles, sem) = refs[2 : 2 + len(fetch)], refs[2 + len(fetch) :]
        tile_refs = [tiles.at[b] for b in range(len(members))]
    member = lax.rem(lax.axis_index("row"), sections)
    odd = member & 1

    def section(slot):
        return member ^ jnp.where(odd > 0, slot[1], slot[0])

    places = [section(slot) for slot in members]
    blocksize = out_ref.shape[0]
    copies = []
    if not has_tiles:
        for slot, target in zip(list(members) + fetch, list(tile_refs) + list(fetch_refs)):
            column = pl.multiple_of(section(slot) * blocksize, PAIR_ROWS)
            copy = pltpu.make_async_copy(
                adjacency_ref.at[:, pl.ds(column, blocksize)], target, sem.at[len(copies)]
            )
            pl.when(live_ref[0, section(slot)] > 0)(copy.start)
            copies.append(copy)
    if has_previous:
        out_ref[...] = previous_ref[...]
    else:
        out_ref[...] = jnp.zeros_like(out_ref)
    at = 0
    for b, rows in enumerate(rows_of):
        pieces = piece_refs[at : at + len(rows)]
        at += len(rows)

        @pl.when(live_ref[0, places[b]] > 0)
        def _():
            if not has_tiles:
                copies[b].wait()
            for piece, to in zip(pieces, rows):
                out_ref[...] += jnp.dot(
                    tile_refs[b][:, to : to + piece.shape[0]],
                    piece[...],
                    preferred_element_type=jnp.float32,
                )

    for slot, copy in zip(fetch, copies[len(members) :]):
        pl.when(live_ref[0, section(slot)] > 0)(copy.wait)


def vmem(count):
    return [pl.BlockSpec(memory_space=pltpu.VMEM)] * count


def aggregate(tile_live, adjacency, blocks, members, previous, tiles=None, fetch=()):
    blocksize = adjacency.shape[0]
    channels = blocks[0][0][0].shape[1]
    fetch = list(fetch)
    pieces = [piece for block in blocks for piece, _ in block]
    rows_of = [[to for _, to in block] for block in blocks]
    extra = [] if previous is None else [previous]
    extra_tiles = [] if tiles is None else list(tiles)
    tile = jax.ShapeDtypeStruct((blocksize, blocksize), adjacency.dtype)
    n_loads = len(members) + len(fetch)
    out = pl.pallas_call(
        functools.partial(
            aggregate_kernel,
            rows_of,
            members,
            fetch,
            adjacency.shape[1] // blocksize,
            tiles is not None,
            previous is not None,
        ),
        in_specs=[pl.BlockSpec(memory_space=pltpu.SMEM)]
        + vmem(len(pieces) + len(extra) + len(extra_tiles))
        + ([pl.BlockSpec(memory_space=pl.ANY)] if tiles is None else []),
        out_specs=vmem(1 + len(fetch)),
        out_shape=[jax.ShapeDtypeStruct((blocksize, channels), jnp.float32)] + [tile] * len(fetch),
        scratch_shapes=[
            pltpu.VMEM((len(members), blocksize, blocksize), adjacency.dtype),
            pltpu.SemaphoreType.DMA((n_loads,)),
        ]
        if tiles is None
        else [],
        compiler_params=pltpu.CompilerParams(
            vmem_limit_bytes=(44 if tiles is None else 8) * 1024 * 1024
        ),
    )(tile_live, *pieces, *extra, *(extra_tiles if tiles is not None else [adjacency]))
    return out[0], out[1:]


def score_kernel(rows_of, which, has_previous, code_ref, ends_ref, emb_ref, *refs):
    n_pieces = sum(len(rows) for rows in rows_of)
    piece_refs, refs = refs[:n_pieces], refs[n_pieces:]
    previous_refs, refs = (refs[:2], refs[2:]) if has_previous else (None, refs)
    pos_ref, neg_ref, scores, losses = refs
    blocksize, channels = emb_ref.shape
    n_pairs = pos_ref.shape[0]
    n_tiles = blocksize // PAIR_ROWS
    if has_previous:
        losses[:n_pairs, :] = previous_refs[0][...]
        losses[n_pairs:, :] = previous_refs[1][...]
    else:
        losses[...] = jnp.zeros_like(losses)
    scores[:, len(rows_of) * blocksize :, :] = jnp.zeros((n_tiles, EDGE, PAIR_ROWS), jnp.float32)
    at = 0
    for b, rows in enumerate(rows_of):
        for piece, to in zip(piece_refs[at : at + len(rows)], rows):
            first = b * blocksize + to
            for t in range(0, n_tiles, WIDE // PAIR_ROWS):
                product = lax.dot_general(
                    piece[...],
                    emb_ref[t * PAIR_ROWS : t * PAIR_ROWS + WIDE, :],
                    (((1,), (1,)), ((), ())),
                    preferred_element_type=jnp.float32,
                )
                for u in range(WIDE // PAIR_ROWS):
                    scores[t + u, first : first + piece.shape[0], :] = product[
                        :, u * PAIR_ROWS : (u + 1) * PAIR_ROWS
                    ]
        at += len(rows)

    row_of = lax.broadcasted_iota(jnp.int32, (EDGE, PAIR_ROWS), 0)
    scale = math.log2(math.e) / math.sqrt(channels)
    first_pair, end_pair = ends_ref[which], ends_ref[which + 1]

    def one_pair(at):
        code = code_ref[at]
        query = code & 7
        first = lax.shift_right_logical(code, 3) & 0x1FFF
        out_row = lax.shift_right_logical(code, 16)
        factor = jnp.where(out_row >= n_pairs, scale, -scale)
        base = pl.multiple_of(first & ~(EDGE - 1), EDGE)
        shift = first & (EDGE - 1)
        window = scores[query, pl.ds(base, PAIR_ROWS + EDGE), :]
        edge = jnp.where(row_of >= shift, window[:EDGE], window[PAIR_ROWS:])
        window = jnp.concatenate([edge, window[EDGE:PAIR_ROWS]], axis=0)
        terms = 1.0 + jnp.exp2(window * factor)
        quarter = PAIR_ROWS // 4
        product = (terms[:quarter] * terms[quarter : 2 * quarter]) * (
            terms[2 * quarter : 3 * quarter] * terms[3 * quarter :]
        )
        return out_row, jnp.sum(jnp.log(product), axis=0, keepdims=True) * (1.0 / PAIR_ROWS)

    def step(i, carry):
        start = first_pair + i * UNROLL
        results = [one_pair(jnp.minimum(start + u, end_pair - 1)) for u in range(UNROLL)]
        for out_row, loss in results:
            losses[pl.ds(out_row, 1), :] = loss
        return carry

    lax.fori_loop(0, lax.div(end_pair - first_pair + (UNROLL - 1), UNROLL), step, 0)
    pos_ref[...] = losses[:n_pairs, :]
    neg_ref[...] = losses[n_pairs:, :]


def score_pairs(codes, ends, which, embedding_block, blocks, n_pairs, previous):
    blocksize, channels = embedding_block.shape
    n_rows = len(blocks) * blocksize
    loss = jax.ShapeDtypeStruct((n_pairs, PAIR_ROWS), jnp.float32)
    pieces = [piece for block in blocks for piece, _ in block]
    rows_of = [[to for _, to in block] for block in blocks]
    extra = [] if previous is None else list(previous)
    return pl.pallas_call(
        functools.partial(score_kernel, rows_of, which, previous is not None),
        in_specs=[pl.BlockSpec(memory_space=pltpu.SMEM)] * 2 + vmem(1 + len(pieces) + len(extra)),
        out_specs=vmem(2),
        scratch_shapes=[
            pltpu.VMEM((blocksize // PAIR_ROWS, n_rows + EDGE, PAIR_ROWS), jnp.float32),
            pltpu.VMEM((2 * n_pairs, PAIR_ROWS), jnp.float32),
        ],
        out_shape=[loss, loss],
        compiler_params=pltpu.CompilerParams(vmem_limit_bytes=24 * 1024 * 1024),
    )(codes, ends, embedding_block, *pieces, *extra)


def order_pairs(pairs, member, sets, blocksize):
    n_all = pairs.shape[0]
    place = pairs[:, 1] ^ member
    in_set = jnp.zeros_like(place)
    at = jnp.zeros_like(place)
    for c, members in enumerate(sets):
        for i, (even, odd) in enumerate(members):
            here = place == jnp.where(member & 1 > 0, odd, even)
            in_set = jnp.where(here, c, in_set)
            at = jnp.where(here, i, at)
    index = jnp.arange(n_all, dtype=jnp.int32)
    code = ((index << 16) | ((at * blocksize + pairs[:, 2]) << 3)) | pairs[:, 0]
    sort_by = in_set * n_all + index
    rank = jnp.sum((sort_by[None, :] < sort_by[:, None]).astype(jnp.int32), axis=1)
    codes = jnp.sum(jnp.where(rank[None, :] == index[:, None], code[None, :], 0), axis=1)
    levels = jnp.arange(len(sets) + 1, dtype=jnp.int32)
    ends = jnp.sum((in_set[None, :] < levels[:, None]).astype(jnp.int32), axis=1)
    return codes, ends


class Spread:
    def __init__(self, n_row, n_rep, sections):
        self.n_row, self.n_rep, self.sections = n_row, n_rep, sections
        self.groups = n_row // sections
        self.rep = lax.axis_index("rep")
        row = lax.axis_index("row")
        self.group, self.member = row // sections, row % sections
        self.everyone = [(r, p) for r in range(n_row) for p in range(n_rep)]
        self.halved = n_rep == 2 and self.groups == 2 and sections == 8
        if self.halved:
            self.slots = [(0, 0), (1, 1), (2, 4), (5, 3), (4, 2), (3, 5), (6, 6), (7, 7)]
            self.sets = [[0, 1], [2, 3, 4, 5], [6], [7]]
        else:
            self.slots = [(j, j) for j in range(sections)]
            self.sets = [list(range(sections))]
        self.members = [[self.slots[slot] for slot in members] for members in self.sets]

    def flip(self, block, stride):
        return permute(
            block, [((r, p), (r ^ stride, p)) for r, p in self.everyone], self.n_rep
        )

    def flip_either(self, block, even, odd):
        return permute(
            block,
            [((r, p), (r ^ (odd if r & 1 else even), p)) for r, p in self.everyone],
            self.n_rep,
        )

    def to_holder(self, block):
        return permute(
            block, [((r, p), (r, r & 1)) for r, p in self.everyone if p != r & 1], self.n_rep
        )

    def from_holder(self, block):
        return permute(
            block, [((r, p), (r, 1 - p)) for r, p in self.everyone if p == r & 1], self.n_rep
        )

    def run_halved(self, held, own, consume):
        n = self.sections
        half = own[0].shape[0]
        across = [
            ((r, p), ((r + n) % self.n_row, r // n)) for r, p in self.everyone if p == r & 1
        ]
        start, near, first, second = [], [], [], []
        came = [permute(part, across, self.n_rep) for part in held]
        for own_part, came_part in zip(own, came):
            part = jnp.where(self.group == self.rep, own_part, came_part)
            start.append(part)
            first.append(self.flip_either(part, 2, 4))
            second.append(self.flip_either(part, 4, 2))
            near.append(self.flip(part, 1))

        def whole(parts):
            return [(part, i * half) for i, part in enumerate(parts)]

        def near_of(parts):
            return [self.flip(part, 1) for part in parts]

        done = consume(0, [whole(start), whole(near)], None)
        first[1], second[1], done = lax.optimization_barrier((first[1], second[1], done))
        third = [self.flip_either(part, 4, 2) for part in first]
        done = consume(
            1,
            [whole(x) for parts in (first, second) for x in (parts, near_of(parts))],
            done,
        )
        third[1], done = lax.optimization_barrier((third[1], done))
        near_third = near_of(third)
        done = consume(2, [whole(third)], done)
        return consume(3, [whole(near_third)], done)

    def run_whole(self, block, consume):
        start = block
        for d in range(1, self.groups):
            came = permute(
                block,
                [
                    ((p * self.sections + m, p), (((p + d) % self.groups) * self.sections + m, p))
                    for p in range(self.n_rep)
                    for m in range(self.sections)
                ],
                self.n_rep,
            )
            start = jnp.where(self.group == (self.rep + d) % self.groups, came, start)
        blocks = {0: start}
        for b in reversed(range(self.sections.bit_length() - 1)):
            for j in list(blocks):
                blocks[j ^ (1 << b)] = self.flip(blocks[j], 1 << b)
        return consume(0, [[(blocks[j], 0)] for j in range(self.sections)], None)


def per_device(
    n_row, n_rep, features, adjacency, tile_live, w_self, w_neigh, bias_vector, pos_pairs, neg_pairs
):
    blocksize = features.shape[0]
    sections = tile_live.shape[1]
    n_pairs = pos_pairs.shape[1]
    share = blocksize // n_rep
    spread = Spread(n_row, n_rep, sections)
    rep, sets = spread.rep, spread.members

    fetched = {}

    def add_tiles(which, blocks, earlier):
        members = sets[which]
        last = [slot for later in sets[2:] for slot in later] if which == 1 else []
        tiles = [fetched[slot] for slot in members] if members[0] in fetched else None
        total, more = aggregate(tile_live, adjacency, blocks, members, earlier, tiles, last)
        fetched.update(zip(last, more))
        return total

    if spread.halved:
        parts = [features[:share], features[share:]]
        partial = spread.run_halved(parts, parts, add_tiles)
    else:
        partial = spread.run_whole(features, add_tiles)

    codes, ends = order_pairs(
        jnp.concatenate([pos_pairs[0], neg_pairs[0]], axis=0), spread.member, sets, blocksize
    )
    def embed(feats, summed):
        projected = jnp.dot(feats, w_self, preferred_element_type=jnp.float32) + bias_vector
        projected = projected + jnp.dot(
            summed.astype(jnp.bfloat16), w_neigh, preferred_element_type=jnp.float32
        )
        scale = lax.rsqrt(jnp.mean(projected * projected, axis=-1, keepdims=True) + 1e-06)
        return (projected * scale).astype(jnp.bfloat16)

    if spread.halved:
        held = []
        for i, feats in enumerate(parts):
            mine = partial[i * share : (i + 1) * share]
            other = spread.to_holder(mine.astype(jnp.bfloat16))
            held.append(embed(feats, mine + other.astype(jnp.float32)))
    else:
        own_feats = lax.dynamic_slice_in_dim(features, rep * share, share, 0)
        embedding = embed(own_feats, lax.psum_scatter(partial, "rep", scatter_dimension=0, tiled=True))

    def score(queries, which, blocks, earlier):
        return score_pairs(codes, ends, which, queries, blocks, n_pairs, earlier)

    if spread.halved:
        holder = rep == spread.member & 1
        own = [jnp.where(holder, part, spread.from_holder(part)) for part in held]
        block = jnp.concatenate(own, axis=0)
        embedding = jnp.where(rep == 0, own[0], own[1])
        losses = spread.run_halved(held, own, functools.partial(score, block))
    else:
        block = lax.all_gather(embedding, "rep", axis=0, tiled=True)
        losses = spread.run_whole(block, functools.partial(score, block))
    return (embedding, losses[0][None], losses[1][None])


def solution(mesh):
    return jax.shard_map(
        functools.partial(per_device, mesh.shape["row"], mesh.shape["rep"]),
        mesh=mesh,
        in_specs=(
            P("row", None),
            P("row", "rep"),
            P("row", "rep"),
            P(),
            P(),
            P(),
            P("row", "rep", None),
            P("row", "rep", None),
        ),
        out_specs=(P(("row", "rep"), None), P("row", "rep", None), P("row", "rep", None)),
        check_vma=False,
    )
```

```python
import functools
import math

import jax
import jax.numpy as jnp
from jax import lax
from jax.experimental import pallas as pl
from jax.experimental.pallas import tpu as pltpu
from jax.sharding import PartitionSpec as P

PAIR_ROWS = 128
EDGE = 8
UNROLL = 8
WIDE = 256


def permute(block, pairs, n_rep):
    return lax.ppermute(
        block, ("row", "rep"), [(a[0] * n_rep + a[1], b[0] * n_rep + b[1]) for a, b in pairs]
    )


def plan(blocks):
    arrays, places = [], []
    for block in blocks:
        places.append([])
        for array, start, to, rows in block:
            at = [i for i, known in enumerate(arrays) if known is array]
            if not at:
                arrays.append(array)
                at = [len(arrays) - 1]
            places[-1].append((at[0], start, to, rows))
    return arrays, places


def whole(parts):
    pieces, to = [], 0
    for part in parts:
        pieces.append((part, 0, to, part.shape[0]))
        to += part.shape[0]
    return pieces


def aggregate_kernel(n_arrays, places, members, fetch, sections, has_tiles, has_previous, live_ref, *refs):
    source_refs, refs = refs[:n_arrays], refs[n_arrays:]
    previous_ref, refs = (refs[0], refs[1:]) if has_previous else (None, refs)
    if has_tiles:
        tile_refs, (out_ref,) = refs[: len(members)], refs[len(members) :]
    else:
        adjacency_ref, out_ref = refs[:2]
        fetch_refs, (tiles, sem) = refs[2 : 2 + len(fetch)], refs[2 + len(fetch) :]
        tile_refs = [tiles.at[b] for b in range(len(members))]
    member = lax.rem(lax.axis_index("row"), sections)
    odd = member & 1

    def section(slot):
        return member ^ jnp.where(odd > 0, slot[1], slot[0])

    sections_of = [section(slot) for slot in members]
    blocksize = out_ref.shape[0]
    copies = []
    if not has_tiles:
        for slot, target in zip(list(members) + fetch, list(tile_refs) + list(fetch_refs)):
            column = pl.multiple_of(section(slot) * blocksize, PAIR_ROWS)
            copy = pltpu.make_async_copy(
                adjacency_ref.at[:, pl.ds(column, blocksize)], target, sem.at[len(copies)]
            )
            pl.when(live_ref[0, section(slot)] > 0)(copy.start)
            copies.append(copy)
    if has_previous:
        out_ref[...] = previous_ref[...]
    else:
        out_ref[...] = jnp.zeros_like(out_ref)
    for b, pieces in enumerate(places):

        @pl.when(live_ref[0, sections_of[b]] > 0)
        def _():
            if not has_tiles:
                copies[b].wait()
            for i, start, to, rows in pieces:
                out_ref[...] += jnp.dot(
                    tile_refs[b][:, to : to + rows],
                    source_refs[i][start : start + rows, :],
                    preferred_element_type=jnp.float32,
                )

    for slot, copy in zip(fetch, copies[len(members) :]):
        pl.when(live_ref[0, section(slot)] > 0)(copy.wait)


def vmem(count):
    return [pl.BlockSpec(memory_space=pltpu.VMEM)] * count


def aggregate(tile_live, adjacency, blocks, members, previous, tiles=None, fetch=()):
    blocksize = adjacency.shape[0]
    channels = blocks[0][0][0].shape[1]
    fetch = list(fetch)
    arrays, places = plan(blocks)
    extra = [] if previous is None else [previous]
    extra_tiles = [] if tiles is None else list(tiles)
    tile = jax.ShapeDtypeStruct((blocksize, blocksize), adjacency.dtype)
    n_loads = len(members) + len(fetch)
    out = pl.pallas_call(
        functools.partial(
            aggregate_kernel,
            len(arrays),
            places,
            members,
            fetch,
            adjacency.shape[1] // blocksize,
            tiles is not None,
            previous is not None,
        ),
        in_specs=[pl.BlockSpec(memory_space=pltpu.SMEM)]
        + vmem(len(arrays) + len(extra) + len(extra_tiles))
        + ([pl.BlockSpec(memory_space=pl.ANY)] if tiles is None else []),
        out_specs=vmem(1 + len(fetch)),
        out_shape=[jax.ShapeDtypeStruct((blocksize, channels), jnp.float32)] + [tile] * len(fetch),
        scratch_shapes=[
            pltpu.VMEM((len(members), blocksize, blocksize), adjacency.dtype),
            pltpu.SemaphoreType.DMA((n_loads,)),
        ]
        if tiles is None
        else [],
        compiler_params=pltpu.CompilerParams(
            vmem_limit_bytes=(44 if tiles is None else 8) * 1024 * 1024
        ),
    )(tile_live, *arrays, *extra, *(extra_tiles if tiles is not None else [adjacency]))
    return out[0], out[1:]


def score_kernel(n_arrays, places, which, has_previous, code_ref, ends_ref, emb_ref, *refs):
    key_refs, refs = refs[:n_arrays], refs[n_arrays:]
    previous_refs, refs = (refs[:2], refs[2:]) if has_previous else (None, refs)
    pos_ref, neg_ref, scores, losses = refs
    blocksize, channels = emb_ref.shape
    n_pairs = pos_ref.shape[0]
    n_tiles = blocksize // PAIR_ROWS
    if has_previous:
        losses[:n_pairs, :] = previous_refs[0][...]
        losses[n_pairs:, :] = previous_refs[1][...]
    else:
        losses[...] = jnp.zeros_like(losses)
    scores[:, len(places) * blocksize :, :] = jnp.zeros((n_tiles, EDGE, PAIR_ROWS), jnp.float32)
    for b, pieces in enumerate(places):
        for i, start, to, rows in pieces:
            first = b * blocksize + to
            for t in range(0, n_tiles, WIDE // PAIR_ROWS):
                product = lax.dot_general(
                    key_refs[i][start : start + rows, :],
                    emb_ref[t * PAIR_ROWS : t * PAIR_ROWS + WIDE, :],
                    (((1,), (1,)), ((), ())),
                    preferred_element_type=jnp.float32,
                )
                for u in range(WIDE // PAIR_ROWS):
                    scores[t + u, first : first + rows, :] = product[
                        :, u * PAIR_ROWS : (u + 1) * PAIR_ROWS
                    ]

    row_of = lax.broadcasted_iota(jnp.int32, (EDGE, PAIR_ROWS), 0)
    scale = math.log2(math.e) / math.sqrt(channels)
    first_pair, end_pair = ends_ref[which], ends_ref[which + 1]

    def one_pair(at):
        code = code_ref[at]
        query = code & 7
        first = lax.shift_right_logical(code, 3) & 0x1FFF
        out_row = lax.shift_right_logical(code, 16)
        factor = jnp.where(out_row >= n_pairs, scale, -scale)
        base = pl.multiple_of(first & ~(EDGE - 1), EDGE)
        shift = first & (EDGE - 1)
        window = scores[query, pl.ds(base, PAIR_ROWS + EDGE), :]
        edge = jnp.where(row_of >= shift, window[:EDGE], window[PAIR_ROWS:])
        window = jnp.concatenate([edge, window[EDGE:PAIR_ROWS]], axis=0)
        terms = 1.0 + jnp.exp2(window * factor)
        quarter = PAIR_ROWS // 4
        product = (terms[:quarter] * terms[quarter : 2 * quarter]) * (
            terms[2 * quarter : 3 * quarter] * terms[3 * quarter :]
        )
        return out_row, jnp.sum(jnp.log(product), axis=0, keepdims=True) * (1.0 / PAIR_ROWS)

    def step(i, carry):
        start = first_pair + i * UNROLL
        results = [one_pair(jnp.minimum(start + u, end_pair - 1)) for u in range(UNROLL)]
        for out_row, loss in results:
            losses[pl.ds(out_row, 1), :] = loss
        return carry

    lax.fori_loop(0, lax.div(end_pair - first_pair + (UNROLL - 1), UNROLL), step, 0)
    pos_ref[...] = losses[:n_pairs, :]
    neg_ref[...] = losses[n_pairs:, :]


def score_pairs(codes, ends, which, embedding_block, blocks, n_pairs, previous):
    blocksize, channels = embedding_block.shape
    n_rows = len(blocks) * blocksize
    loss = jax.ShapeDtypeStruct((n_pairs, PAIR_ROWS), jnp.float32)
    arrays, places = plan(blocks)
    extra = [] if previous is None else list(previous)
    return pl.pallas_call(
        functools.partial(score_kernel, len(arrays), places, which, previous is not None),
        in_specs=[pl.BlockSpec(memory_space=pltpu.SMEM)] * 2 + vmem(1 + len(arrays) + len(extra)),
        out_specs=vmem(2),
        scratch_shapes=[
            pltpu.VMEM((blocksize // PAIR_ROWS, n_rows + EDGE, PAIR_ROWS), jnp.float32),
            pltpu.VMEM((2 * n_pairs, PAIR_ROWS), jnp.float32),
        ],
        out_shape=[loss, loss],
        compiler_params=pltpu.CompilerParams(vmem_limit_bytes=24 * 1024 * 1024),
    )(codes, ends, embedding_block, *arrays, *extra)


def order_pairs(pairs, member, sets, blocksize):
    n_all = pairs.shape[0]
    place = pairs[:, 1] ^ member
    in_set = jnp.zeros_like(place)
    at = jnp.zeros_like(place)
    for c, members in enumerate(sets):
        for i, (even, odd) in enumerate(members):
            here = place == jnp.where(member & 1 > 0, odd, even)
            in_set = jnp.where(here, c, in_set)
            at = jnp.where(here, i, at)
    index = jnp.arange(n_all, dtype=jnp.int32)
    code = ((index << 16) | ((at * blocksize + pairs[:, 2]) << 3)) | pairs[:, 0]
    sort_by = in_set * n_all + index
    rank = jnp.sum((sort_by[None, :] < sort_by[:, None]).astype(jnp.int32), axis=1)
    codes = jnp.sum(jnp.where(rank[None, :] == index[:, None], code[None, :], 0), axis=1)
    levels = jnp.arange(len(sets) + 1, dtype=jnp.int32)
    ends = jnp.sum((in_set[None, :] < levels[:, None]).astype(jnp.int32), axis=1)
    return codes, ends


class Spread:
    def __init__(self, n_row, n_rep, sections):
        self.n_row, self.n_rep, self.sections = n_row, n_rep, sections
        self.groups = n_row // sections
        self.rep = lax.axis_index("rep")
        row = lax.axis_index("row")
        self.group, self.member = row // sections, row % sections
        self.everyone = [(r, p) for r in range(n_row) for p in range(n_rep)]
        self.halved = n_rep == 2 and self.groups == 2 and sections == 8
        if self.halved:
            self.slots = [(0, 0), (1, 1), (2, 4), (5, 3), (4, 2), (3, 5), (6, 6), (7, 7)]
        else:
            self.slots = [(j, j) for j in range(sections)]

    def flip(self, block, stride):
        return permute(
            block, [((r, p), (r ^ stride, p)) for r, p in self.everyone], self.n_rep
        )

    def flip_either(self, block, even, odd):
        return permute(
            block,
            [((r, p), (r ^ (odd if r & 1 else even), p)) for r, p in self.everyone],
            self.n_rep,
        )

    def swap(self, block):
        return permute(block, [((r, p), (r, 1 - p)) for r, p in self.everyone], self.n_rep)

    def run_halved(self, parts, consume):
        n = self.sections
        across = [
            ((r, p), ((r + n) % self.n_row, r // n)) for r, p in self.everyone if p == r & 1
        ]
        came = [permute(part, across, self.n_rep) for part in parts]
        start = [jnp.where(self.group == self.rep, x, y) for x, y in zip(parts, came)]
        first = [self.flip_either(part, 2, 4) for part in start]
        second = [self.flip_either(part, 4, 2) for part in start]
        near = [self.flip(part, 1) for part in start]
        done = consume([whole(start), whole(near)], None)
        halves = first
        if len(first) == 1:
            half = first[0].shape[0] // 2
            halves = [first[0][:half], first[0][half:]]
        third = [self.flip_either(part, 4, 2) for part in halves]
        near_first = [self.flip(part, 1) for part in first]
        near_second = [self.flip(part, 1) for part in second]
        done = consume([whole(x) for x in (first, near_first, second, near_second)], done)
        third[1], done = lax.optimization_barrier((third[1], done))
        if len(first) == 1:
            third[0], done = lax.optimization_barrier((third[0], done))
        near_third = [self.flip(part, 1) for part in third]
        done = consume([whole(third)], done)
        return consume([whole(near_third)], done)

    def run_whole(self, block, consume):
        start = block
        for d in range(1, self.groups):
            came = permute(
                block,
                [
                    ((p * self.sections + m, p), (((p + d) % self.groups) * self.sections + m, p))
                    for p in range(self.n_rep)
                    for m in range(self.sections)
                ],
                self.n_rep,
            )
            start = jnp.where(self.group == (self.rep + d) % self.groups, came, start)
        blocks = {0: start}
        for b in reversed(range(self.sections.bit_length() - 1)):
            for j in list(blocks):
                blocks[j ^ (1 << b)] = self.flip(blocks[j], 1 << b)
        return consume([whole([blocks[j]]) for j in range(self.sections)], None)


def per_device(
    n_row, n_rep, features, adjacency, tile_live, w_self, w_neigh, bias_vector, pos_pairs, neg_pairs
):
    blocksize = features.shape[0]
    sections = tile_live.shape[1]
    n_pairs = pos_pairs.shape[1]
    share = blocksize // n_rep
    spread = Spread(n_row, n_rep, sections)
    rep, slots = spread.rep, spread.slots

    fetched, added = {}, []

    def add_tiles(blocks, earlier):
        members = slots[len(added) : len(added) + len(blocks)]
        added.extend(members)
        left = slots[len(added) :]
        last = left if 0 < len(left) <= 2 and not fetched else []
        tiles = [fetched[slot] for slot in members] if members[0] in fetched else None
        total, more = aggregate(tile_live, adjacency, blocks, members, earlier, tiles, last)
        fetched.update(zip(last, more))
        return total

    if spread.halved:
        partial = spread.run_halved([features], add_tiles)
    else:
        partial = spread.run_whole(features, add_tiles)

    sets = [slots[:2], slots[2:6], [slots[6]], [slots[7]]] if spread.halved else [slots]
    codes, ends = order_pairs(
        jnp.concatenate([pos_pairs[0], neg_pairs[0]], axis=0), spread.member, sets, blocksize
    )
    def embed(feats, summed):
        projected = jnp.dot(feats, w_self, preferred_element_type=jnp.float32) + bias_vector
        projected = projected + jnp.dot(
            summed.astype(jnp.bfloat16), w_neigh, preferred_element_type=jnp.float32
        )
        scale = lax.rsqrt(jnp.mean(projected * projected, axis=-1, keepdims=True) + 1e-06)
        return (projected * scale).astype(jnp.bfloat16)

    if spread.halved:
        own = []
        for i in range(2):
            rows = slice(i * share, (i + 1) * share)
            other = spread.swap(partial[rows].astype(jnp.bfloat16))
            own.append(embed(features[rows], partial[rows] + other.astype(jnp.float32)))
    else:
        own_feats = lax.dynamic_slice_in_dim(features, rep * share, share, 0)
        embedding = embed(own_feats, lax.psum_scatter(partial, "rep", scatter_dimension=0, tiled=True))

    scored, output = [], []

    def score(queries, blocks, earlier):
        if len(scored) == 1:
            own_now, earlier = lax.optimization_barrier((own, earlier))
            rows = jnp.where(rep == 0, own_now[0], own_now[1])
            rows, earlier = lax.optimization_barrier((rows, earlier))
            output.append(rows)
        scored.append(len(blocks))
        return score_pairs(codes, ends, len(scored) - 1, queries, blocks, n_pairs, earlier)

    if spread.halved:
        block = jnp.concatenate(own, axis=0)
        losses = spread.run_halved(own, functools.partial(score, block))
        embedding = output[0]
    else:
        block = lax.all_gather(embedding, "rep", axis=0, tiled=True)
        losses = spread.run_whole(block, functools.partial(score, block))
    return (embedding, losses[0][None], losses[1][None])


def solution(mesh):
    return jax.shard_map(
        functools.partial(per_device, mesh.shape["row"], mesh.shape["rep"]),
        mesh=mesh,
        in_specs=(
            P("row", None),
            P("row", "rep"),
            P("row", "rep"),
            P(),
            P(),
            P(),
            P("row", "rep", None),
            P("row", "rep", None),
        ),
        out_specs=(P(("row", "rep"), None), P("row", "rep", None), P("row", "rep", None)),
        check_vma=False,
    )
```

```python
import functools
import math

import jax
import jax.numpy as jnp
from jax import lax
from jax.experimental import pallas as pl
from jax.experimental.pallas import tpu as pltpu
from jax.sharding import PartitionSpec as P

PAIR_ROWS = 128
EDGE = 8
UNROLL = 8
WIDE = 256


def permute(block, pairs, n_rep):
    return lax.ppermute(
        block, ("row", "rep"), [(a[0] * n_rep + a[1], b[0] * n_rep + b[1]) for a, b in pairs]
    )


def plan(blocks):
    arrays, places = [], []
    for block in blocks:
        places.append([])
        for array, start, to, rows in block:
            at = [i for i, known in enumerate(arrays) if known is array]
            if not at:
                arrays.append(array)
                at = [len(arrays) - 1]
            places[-1].append((at[0], start, to, rows))
    return arrays, places


def whole(parts):
    pieces, to = [], 0
    for part in parts:
        pieces.append((part, 0, to, part.shape[0]))
        to += part.shape[0]
    return pieces


def aggregate_kernel(n_arrays, places, members, fetch, sections, has_tiles, has_previous, live_ref, *refs):
    source_refs, refs = refs[:n_arrays], refs[n_arrays:]
    previous_ref, refs = (refs[0], refs[1:]) if has_previous else (None, refs)
    if has_tiles:
        tile_refs, (out_ref,) = refs[: len(members)], refs[len(members) :]
    else:
        adjacency_ref, out_ref = refs[:2]
        fetch_refs, (tiles, sem) = refs[2 : 2 + len(fetch)], refs[2 + len(fetch) :]
        tile_refs = [tiles.at[b] for b in range(len(members))]
    member = lax.rem(lax.axis_index("row"), sections)
    odd = member & 1

    def section(slot):
        return member ^ jnp.where(odd > 0, slot[1], slot[0])

    sections_of = [section(slot) for slot in members]
    blocksize = out_ref.shape[0]
    copies = []
    if not has_tiles:
        for slot, target in zip(list(members) + fetch, list(tile_refs) + list(fetch_refs)):
            column = pl.multiple_of(section(slot) * blocksize, PAIR_ROWS)
            copy = pltpu.make_async_copy(
                adjacency_ref.at[:, pl.ds(column, blocksize)], target, sem.at[len(copies)]
            )
            pl.when(live_ref[0, section(slot)] > 0)(copy.start)
            copies.append(copy)
    if has_previous:
        out_ref[...] = previous_ref[...]
    else:
        out_ref[...] = jnp.zeros_like(out_ref)
    for b, pieces in enumerate(places):

        @pl.when(live_ref[0, sections_of[b]] > 0)
        def _():
            if not has_tiles:
                copies[b].wait()
            for i, start, to, rows in pieces:
                out_ref[...] += jnp.dot(
                    tile_refs[b][:, to : to + rows],
                    source_refs[i][start : start + rows, :],
                    preferred_element_type=jnp.float32,
                )

    for slot, copy in zip(fetch, copies[len(members) :]):
        pl.when(live_ref[0, section(slot)] > 0)(copy.wait)


def vmem(count):
    return [pl.BlockSpec(memory_space=pltpu.VMEM)] * count


def aggregate(tile_live, adjacency, blocks, members, previous, tiles=None, fetch=()):
    blocksize = adjacency.shape[0]
    channels = blocks[0][0][0].shape[1]
    fetch = list(fetch)
    arrays, places = plan(blocks)
    extra = [] if previous is None else [previous]
    extra_tiles = [] if tiles is None else list(tiles)
    tile = jax.ShapeDtypeStruct((blocksize, blocksize), adjacency.dtype)
    n_loads = len(members) + len(fetch)
    out = pl.pallas_call(
        functools.partial(
            aggregate_kernel,
            len(arrays),
            places,
            members,
            fetch,
            adjacency.shape[1] // blocksize,
            tiles is not None,
            previous is not None,
        ),
        in_specs=[pl.BlockSpec(memory_space=pltpu.SMEM)]
        + vmem(len(arrays) + len(extra) + len(extra_tiles))
        + ([pl.BlockSpec(memory_space=pl.ANY)] if tiles is None else []),
        out_specs=vmem(1 + len(fetch)),
        out_shape=[jax.ShapeDtypeStruct((blocksize, channels), jnp.float32)] + [tile] * len(fetch),
        scratch_shapes=[
            pltpu.VMEM((len(members), blocksize, blocksize), adjacency.dtype),
            pltpu.SemaphoreType.DMA((n_loads,)),
        ]
        if tiles is None
        else [],
        compiler_params=pltpu.CompilerParams(
            vmem_limit_bytes=(44 if tiles is None else 8) * 1024 * 1024
        ),
    )(tile_live, *arrays, *extra, *(extra_tiles if tiles is not None else [adjacency]))
    return out[0], out[1:]


def score_kernel(n_arrays, places, which, has_previous, write_rows, code_ref, ends_ref, emb_ref, *refs):
    key_refs, refs = refs[:n_arrays], refs[n_arrays:]
    previous_refs, refs = (refs[:2], refs[2:]) if has_previous else (None, refs)
    if write_rows:
        rows_ref, refs = refs[0], refs[1:]
        first = pl.multiple_of(lax.axis_index("rep") * write_rows, PAIR_ROWS)
        rows_ref[...] = emb_ref[pl.ds(first, write_rows), :]
    pos_ref, neg_ref, scores, losses = refs
    blocksize, channels = emb_ref.shape
    n_pairs = pos_ref.shape[0]
    n_tiles = blocksize // PAIR_ROWS
    if has_previous:
        losses[:n_pairs, :] = previous_refs[0][...]
        losses[n_pairs:, :] = previous_refs[1][...]
    else:
        losses[...] = jnp.zeros_like(losses)
    scores[:, len(places) * blocksize :, :] = jnp.zeros((n_tiles, EDGE, PAIR_ROWS), jnp.float32)
    for b, pieces in enumerate(places):
        for i, start, to, rows in pieces:
            first = b * blocksize + to
            for t in range(0, n_tiles, WIDE // PAIR_ROWS):
                product = lax.dot_general(
                    key_refs[i][start : start + rows, :],
                    emb_ref[t * PAIR_ROWS : t * PAIR_ROWS + WIDE, :],
                    (((1,), (1,)), ((), ())),
                    preferred_element_type=jnp.float32,
                )
                for u in range(WIDE // PAIR_ROWS):
                    scores[t + u, first : first + rows, :] = product[
                        :, u * PAIR_ROWS : (u + 1) * PAIR_ROWS
                    ]

    row_of = lax.broadcasted_iota(jnp.int32, (EDGE, PAIR_ROWS), 0)
    scale = math.log2(math.e) / math.sqrt(channels)
    first_pair, end_pair = ends_ref[which], ends_ref[which + 1]

    def one_pair(at):
        code = code_ref[at]
        query = code & 7
        first = lax.shift_right_logical(code, 3) & 0x1FFF
        out_row = lax.shift_right_logical(code, 16)
        factor = jnp.where(out_row >= n_pairs, scale, -scale)
        base = pl.multiple_of(first & ~(EDGE - 1), EDGE)
        shift = first & (EDGE - 1)
        window = scores[query, pl.ds(base, PAIR_ROWS + EDGE), :]
        edge = jnp.where(row_of >= shift, window[:EDGE], window[PAIR_ROWS:])
        window = jnp.concatenate([edge, window[EDGE:PAIR_ROWS]], axis=0)
        terms = 1.0 + jnp.exp2(window * factor)
        quarter = PAIR_ROWS // 4
        product = (terms[:quarter] * terms[quarter : 2 * quarter]) * (
            terms[2 * quarter : 3 * quarter] * terms[3 * quarter :]
        )
        return out_row, jnp.sum(jnp.log(product), axis=0, keepdims=True) * (1.0 / PAIR_ROWS)

    def step(i, carry):
        start = first_pair + i * UNROLL
        results = [one_pair(jnp.minimum(start + u, end_pair - 1)) for u in range(UNROLL)]
        for out_row, loss in results:
            losses[pl.ds(out_row, 1), :] = loss
        return carry

    lax.fori_loop(0, lax.div(end_pair - first_pair + (UNROLL - 1), UNROLL), step, 0)
    pos_ref[...] = losses[:n_pairs, :]
    neg_ref[...] = losses[n_pairs:, :]


def score_pairs(codes, ends, which, embedding_block, blocks, n_pairs, previous, write_rows=0):
    blocksize, channels = embedding_block.shape
    n_rows = len(blocks) * blocksize
    loss = jax.ShapeDtypeStruct((n_pairs, PAIR_ROWS), jnp.float32)
    rows = [jax.ShapeDtypeStruct((write_rows, channels), jnp.bfloat16)] if write_rows else []
    arrays, places = plan(blocks)
    extra = [] if previous is None else list(previous)
    return pl.pallas_call(
        functools.partial(score_kernel, len(arrays), places, which, previous is not None, write_rows),
        in_specs=[pl.BlockSpec(memory_space=pltpu.SMEM)] * 2 + vmem(1 + len(arrays) + len(extra)),
        out_specs=vmem(2 + len(rows)),
        scratch_shapes=[
            pltpu.VMEM((blocksize // PAIR_ROWS, n_rows + EDGE, PAIR_ROWS), jnp.float32),
            pltpu.VMEM((2 * n_pairs, PAIR_ROWS), jnp.float32),
        ],
        out_shape=rows + [loss, loss],
        compiler_params=pltpu.CompilerParams(vmem_limit_bytes=24 * 1024 * 1024),
    )(codes, ends, embedding_block, *arrays, *extra)


def order_pairs(pairs, member, sets, blocksize):
    n_all = pairs.shape[0]
    place = pairs[:, 1] ^ member
    in_set = jnp.zeros_like(place)
    at = jnp.zeros_like(place)
    for c, members in enumerate(sets):
        for i, (even, odd) in enumerate(members):
            here = place == jnp.where(member & 1 > 0, odd, even)
            in_set = jnp.where(here, c, in_set)
            at = jnp.where(here, i, at)
    index = jnp.arange(n_all, dtype=jnp.int32)
    code = ((index << 16) | ((at * blocksize + pairs[:, 2]) << 3)) | pairs[:, 0]
    sort_by = in_set * n_all + index
    rank = jnp.sum((sort_by[None, :] < sort_by[:, None]).astype(jnp.int32), axis=1)
    codes = jnp.sum(jnp.where(rank[None, :] == index[:, None], code[None, :], 0), axis=1)
    levels = jnp.arange(len(sets) + 1, dtype=jnp.int32)
    ends = jnp.sum((in_set[None, :] < levels[:, None]).astype(jnp.int32), axis=1)
    return codes, ends


class Spread:
    def __init__(self, n_row, n_rep, sections):
        self.n_row, self.n_rep, self.sections = n_row, n_rep, sections
        self.groups = n_row // sections
        self.rep = lax.axis_index("rep")
        row = lax.axis_index("row")
        self.group, self.member = row // sections, row % sections
        self.everyone = [(r, p) for r in range(n_row) for p in range(n_rep)]
        self.halved = n_rep == 2 and self.groups == 2 and sections == 8
        if self.halved:
            self.slots = [(0, 0), (1, 1), (2, 4), (5, 3), (4, 2), (3, 5), (6, 6), (7, 7)]
        else:
            self.slots = [(j, j) for j in range(sections)]

    def flip(self, block, stride):
        return permute(
            block, [((r, p), (r ^ stride, p)) for r, p in self.everyone], self.n_rep
        )

    def flip_either(self, block, even, odd):
        return permute(
            block,
            [((r, p), (r ^ (odd if r & 1 else even), p)) for r, p in self.everyone],
            self.n_rep,
        )

    def swap(self, block):
        return permute(block, [((r, p), (r, 1 - p)) for r, p in self.everyone], self.n_rep)

    def run_halved(self, parts, consume):
        n = self.sections
        across = [
            ((r, p), ((r + n) % self.n_row, r // n)) for r, p in self.everyone if p == r & 1
        ]
        came = [permute(part, across, self.n_rep) for part in parts]
        start = [jnp.where(self.group == self.rep, x, y) for x, y in zip(parts, came)]
        first = [self.flip_either(part, 2, 4) for part in start]
        second = [self.flip_either(part, 4, 2) for part in start]
        near = [self.flip(part, 1) for part in start]
        done = consume([whole(start), whole(near)], None)
        halves = first
        if len(first) == 1:
            half = first[0].shape[0] // 2
            halves = [first[0][:half], first[0][half:]]
        third = [self.flip_either(part, 4, 2) for part in halves]
        near_first = [self.flip(part, 1) for part in first]
        near_second = [self.flip(part, 1) for part in second]
        done = consume([whole(x) for x in (first, near_first, second, near_second)], done)
        third[1], done = lax.optimization_barrier((third[1], done))
        if len(first) == 1:
            third[0], done = lax.optimization_barrier((third[0], done))
        near_third = [self.flip(part, 1) for part in third]
        done = consume([whole(third)], done)
        return consume([whole(near_third)], done)

    def run_whole(self, block, consume):
        start = block
        for d in range(1, self.groups):
            came = permute(
                block,
                [
                    ((p * self.sections + m, p), (((p + d) % self.groups) * self.sections + m, p))
                    for p in range(self.n_rep)
                    for m in range(self.sections)
                ],
                self.n_rep,
            )
            start = jnp.where(self.group == (self.rep + d) % self.groups, came, start)
        blocks = {0: start}
        for b in reversed(range(self.sections.bit_length() - 1)):
            for j in list(blocks):
                blocks[j ^ (1 << b)] = self.flip(blocks[j], 1 << b)
        return consume([whole([blocks[j]]) for j in range(self.sections)], None)


def per_device(
    n_row, n_rep, features, adjacency, tile_live, w_self, w_neigh, bias_vector, pos_pairs, neg_pairs
):
    blocksize = features.shape[0]
    sections = tile_live.shape[1]
    n_pairs = pos_pairs.shape[1]
    share = blocksize // n_rep
    spread = Spread(n_row, n_rep, sections)
    rep, slots = spread.rep, spread.slots

    fetched, added = {}, []

    def add_tiles(blocks, earlier):
        members = slots[len(added) : len(added) + len(blocks)]
        added.extend(members)
        left = slots[len(added) :]
        last = left if 0 < len(left) <= 2 and not fetched else []
        tiles = [fetched[slot] for slot in members] if members[0] in fetched else None
        total, more = aggregate(tile_live, adjacency, blocks, members, earlier, tiles, last)
        fetched.update(zip(last, more))
        return total

    if spread.halved:
        partial = spread.run_halved([features], add_tiles)
    else:
        partial = spread.run_whole(features, add_tiles)

    sets = [slots[:2], slots[2:6], [slots[6]], [slots[7]]] if spread.halved else [slots]
    codes, ends = order_pairs(
        jnp.concatenate([pos_pairs[0], neg_pairs[0]], axis=0), spread.member, sets, blocksize
    )
    def embed(feats, summed):
        projected = jnp.dot(feats, w_self, preferred_element_type=jnp.float32) + bias_vector
        projected = projected + jnp.dot(
            summed.astype(jnp.bfloat16), w_neigh, preferred_element_type=jnp.float32
        )
        scale = lax.rsqrt(jnp.mean(projected * projected, axis=-1, keepdims=True) + 1e-06)
        return (projected * scale).astype(jnp.bfloat16)

    if spread.halved:
        own = []
        for i in range(2):
            rows = slice(i * share, (i + 1) * share)
            other = spread.swap(partial[rows].astype(jnp.bfloat16))
            own.append(embed(features[rows], partial[rows] + other.astype(jnp.float32)))
    else:
        own_feats = lax.dynamic_slice_in_dim(features, rep * share, share, 0)
        embedding = embed(own_feats, lax.psum_scatter(partial, "rep", scatter_dimension=0, tiled=True))

    scored, output = [], []

    def score(queries, blocks, earlier):
        limits = ends
        if len(scored) == 1:
            limits, earlier = lax.optimization_barrier((ends, earlier))
            limits, earlier = lax.optimization_barrier((jnp.maximum(limits, 0), earlier))
        scored.append(len(blocks))
        write_rows = share if spread.halved and len(scored) == 1 else 0
        *rows, pos_loss, neg_loss = score_pairs(
            codes, limits, len(scored) - 1, queries, blocks, n_pairs, earlier, write_rows
        )
        output.extend(rows)
        return pos_loss, neg_loss

    if spread.halved:
        block = jnp.concatenate(own, axis=0)
        losses = spread.run_halved(own, functools.partial(score, block))
        embedding = output[0]
    else:
        block = lax.all_gather(embedding, "rep", axis=0, tiled=True)
        losses = spread.run_whole(block, functools.partial(score, block))
    return (embedding, losses[0][None], losses[1][None])


def solution(mesh):
    return jax.shard_map(
        functools.partial(per_device, mesh.shape["row"], mesh.shape["rep"]),
        mesh=mesh,
        in_specs=(
            P("row", None),
            P("row", "rep"),
            P("row", "rep"),
            P(),
            P(),
            P(),
            P("row", "rep", None),
            P("row", "rep", None),
        ),
        out_specs=(P(("row", "rep"), None), P("row", "rep", None), P("row", "rep", None)),
        check_vma=False,
    )
```

```python
import functools
import math

import jax
import jax.numpy as jnp
from jax import lax
from jax.experimental import pallas as pl
from jax.experimental.pallas import tpu as pltpu
from jax.sharding import PartitionSpec as P

PAIR_ROWS = 128
EDGE = 8
UNROLL = 16
WIDE = 256


def permute(block, pairs, n_rep):
    return lax.ppermute(
        block, ("row", "rep"), [(a[0] * n_rep + a[1], b[0] * n_rep + b[1]) for a, b in pairs]
    )


def plan(blocks):
    arrays, places = [], []
    for block in blocks:
        places.append([])
        for array, start, to, rows in block:
            at = [i for i, known in enumerate(arrays) if known is array]
            if not at:
                arrays.append(array)
                at = [len(arrays) - 1]
            places[-1].append((at[0], start, to, rows))
    return arrays, places


def whole(parts):
    pieces, to = [], 0
    for part in parts:
        pieces.append((part, 0, to, part.shape[0]))
        to += part.shape[0]
    return pieces


def aggregate_kernel(n_arrays, places, members, fetch, sections, has_tiles, has_previous, live_ref, *refs):
    source_refs, refs = refs[:n_arrays], refs[n_arrays:]
    previous_ref, refs = (refs[0], refs[1:]) if has_previous else (None, refs)
    if has_tiles:
        tile_refs, (out_ref,) = refs[: len(members)], refs[len(members) :]
    else:
        adjacency_ref, out_ref = refs[:2]
        fetch_refs, (tiles, sem) = refs[2 : 2 + len(fetch)], refs[2 + len(fetch) :]
        tile_refs = [tiles.at[b] for b in range(len(members))]
    member = lax.rem(lax.axis_index("row"), sections)
    odd = member & 1

    def section(slot):
        return member ^ jnp.where(odd > 0, slot[1], slot[0])

    sections_of = [section(slot) for slot in members]
    blocksize = out_ref.shape[0]
    copies = []
    if not has_tiles:
        for slot, target in zip(list(members) + fetch, list(tile_refs) + list(fetch_refs)):
            column = pl.multiple_of(section(slot) * blocksize, PAIR_ROWS)
            copy = pltpu.make_async_copy(
                adjacency_ref.at[:, pl.ds(column, blocksize)], target, sem.at[len(copies)]
            )
            pl.when(live_ref[0, section(slot)] > 0)(copy.start)
            copies.append(copy)
    if has_previous:
        out_ref[...] = previous_ref[...]
    else:
        out_ref[...] = jnp.zeros_like(out_ref)
    for b, pieces in enumerate(places):

        @pl.when(live_ref[0, sections_of[b]] > 0)
        def _():
            if not has_tiles:
                copies[b].wait()
            for i, start, to, rows in pieces:
                out_ref[...] += jnp.dot(
                    tile_refs[b][:, to : to + rows],
                    source_refs[i][start : start + rows, :],
                    preferred_element_type=jnp.float32,
                )

    for slot, copy in zip(fetch, copies[len(members) :]):
        pl.when(live_ref[0, section(slot)] > 0)(copy.wait)


def vmem(count):
    return [pl.BlockSpec(memory_space=pltpu.VMEM)] * count


def aggregate(tile_live, adjacency, blocks, members, previous, tiles=None, fetch=()):
    blocksize = adjacency.shape[0]
    channels = blocks[0][0][0].shape[1]
    fetch = list(fetch)
    arrays, places = plan(blocks)
    extra = [] if previous is None else [previous]
    extra_tiles = [] if tiles is None else list(tiles)
    tile = jax.ShapeDtypeStruct((blocksize, blocksize), adjacency.dtype)
    n_loads = len(members) + len(fetch)
    out = pl.pallas_call(
        functools.partial(
            aggregate_kernel,
            len(arrays),
            places,
            members,
            fetch,
            adjacency.shape[1] // blocksize,
            tiles is not None,
            previous is not None,
        ),
        in_specs=[pl.BlockSpec(memory_space=pltpu.SMEM)]
        + vmem(len(arrays) + len(extra) + len(extra_tiles))
        + ([pl.BlockSpec(memory_space=pl.ANY)] if tiles is None else []),
        out_specs=vmem(1 + len(fetch)),
        out_shape=[jax.ShapeDtypeStruct((blocksize, channels), jnp.float32)] + [tile] * len(fetch),
        scratch_shapes=[
            pltpu.VMEM((len(members), blocksize, blocksize), adjacency.dtype),
            pltpu.SemaphoreType.DMA((n_loads,)),
        ]
        if tiles is None
        else [],
        compiler_params=pltpu.CompilerParams(
            vmem_limit_bytes=(44 if tiles is None else 8) * 1024 * 1024
        ),
    )(tile_live, *arrays, *extra, *(extra_tiles if tiles is not None else [adjacency]))
    return out[0], out[1:]


def score_kernel(n_arrays, places, which, has_previous, write_rows, code_ref, ends_ref, emb_ref, *refs):
    key_refs, refs = refs[:n_arrays], refs[n_arrays:]
    previous_refs, refs = (refs[:2], refs[2:]) if has_previous else (None, refs)
    if write_rows:
        rows_ref, refs = refs[0], refs[1:]
        first = pl.multiple_of(lax.axis_index("rep") * write_rows, PAIR_ROWS)
        rows_ref[...] = emb_ref[pl.ds(first, write_rows), :]
    pos_ref, neg_ref, scores, losses = refs
    blocksize, channels = emb_ref.shape
    n_pairs = pos_ref.shape[0]
    n_tiles = blocksize // PAIR_ROWS
    if has_previous:
        losses[:n_pairs, :] = previous_refs[0][...]
        losses[n_pairs:, :] = previous_refs[1][...]
    else:
        losses[...] = jnp.zeros_like(losses)
    scores[:, len(places) * blocksize :, :] = jnp.zeros((n_tiles, EDGE, PAIR_ROWS), jnp.float32)
    for b, pieces in enumerate(places):
        for i, start, to, rows in pieces:
            first = b * blocksize + to
            for t in range(0, n_tiles, WIDE // PAIR_ROWS):
                product = lax.dot_general(
                    key_refs[i][start : start + rows, :],
                    emb_ref[t * PAIR_ROWS : t * PAIR_ROWS + WIDE, :],
                    (((1,), (1,)), ((), ())),
                    preferred_element_type=jnp.float32,
                )
                for u in range(WIDE // PAIR_ROWS):
                    scores[t + u, first : first + rows, :] = product[
                        :, u * PAIR_ROWS : (u + 1) * PAIR_ROWS
                    ]

    row_of = lax.broadcasted_iota(jnp.int32, (EDGE, PAIR_ROWS), 0)
    scale = math.log2(math.e) / math.sqrt(channels)
    first_pair, end_pair = ends_ref[which], ends_ref[which + 1]

    def one_pair(at):
        code = code_ref[at]
        query = code & 7
        first = lax.shift_right_logical(code, 3) & 0x1FFF
        out_row = lax.shift_right_logical(code, 16)
        factor = jnp.where(out_row >= n_pairs, scale, -scale)
        base = pl.multiple_of(first & ~(EDGE - 1), EDGE)
        shift = first & (EDGE - 1)
        window = scores[query, pl.ds(base, PAIR_ROWS + EDGE), :]
        edge = jnp.where(row_of >= shift, window[:EDGE], window[PAIR_ROWS:])
        window = jnp.concatenate([edge, window[EDGE:PAIR_ROWS]], axis=0)
        terms = 1.0 + jnp.exp2(window * factor)
        quarter = PAIR_ROWS // 4
        product = (terms[:quarter] * terms[quarter : 2 * quarter]) * (
            terms[2 * quarter : 3 * quarter] * terms[3 * quarter :]
        )
        return out_row, jnp.sum(jnp.log(product), axis=0, keepdims=True) * (1.0 / PAIR_ROWS)

    def step(i, carry):
        start = first_pair + i * UNROLL
        results = [one_pair(jnp.minimum(start + u, end_pair - 1)) for u in range(UNROLL)]
        for out_row, loss in results:
            losses[pl.ds(out_row, 1), :] = loss
        return carry

    lax.fori_loop(0, lax.div(end_pair - first_pair + (UNROLL - 1), UNROLL), step, 0)
    pos_ref[...] = losses[:n_pairs, :]
    neg_ref[...] = losses[n_pairs:, :]


def score_pairs(codes, ends, which, embedding_block, blocks, n_pairs, previous, write_rows=0):
    blocksize, channels = embedding_block.shape
    n_rows = len(blocks) * blocksize
    loss = jax.ShapeDtypeStruct((n_pairs, PAIR_ROWS), jnp.float32)
    rows = [jax.ShapeDtypeStruct((write_rows, channels), jnp.bfloat16)] if write_rows else []
    arrays, places = plan(blocks)
    extra = [] if previous is None else list(previous)
    return pl.pallas_call(
        functools.partial(score_kernel, len(arrays), places, which, previous is not None, write_rows),
        in_specs=[pl.BlockSpec(memory_space=pltpu.SMEM)] * 2 + vmem(1 + len(arrays) + len(extra)),
        out_specs=vmem(2 + len(rows)),
        scratch_shapes=[
            pltpu.VMEM((blocksize // PAIR_ROWS, n_rows + EDGE, PAIR_ROWS), jnp.float32),
            pltpu.VMEM((2 * n_pairs, PAIR_ROWS), jnp.float32),
        ],
        out_shape=rows + [loss, loss],
        compiler_params=pltpu.CompilerParams(vmem_limit_bytes=24 * 1024 * 1024),
    )(codes, ends, embedding_block, *arrays, *extra)


def order_pairs(pairs, member, sets, blocksize):
    n_all = pairs.shape[0]
    place = pairs[:, 1] ^ member
    in_set = jnp.zeros_like(place)
    at = jnp.zeros_like(place)
    for c, members in enumerate(sets):
        for i, (even, odd) in enumerate(members):
            here = place == jnp.where(member & 1 > 0, odd, even)
            in_set = jnp.where(here, c, in_set)
            at = jnp.where(here, i, at)
    index = jnp.arange(n_all, dtype=jnp.int32)
    code = ((index << 16) | ((at * blocksize + pairs[:, 2]) << 3)) | pairs[:, 0]
    sort_by = in_set * n_all + index
    rank = jnp.sum((sort_by[None, :] < sort_by[:, None]).astype(jnp.int32), axis=1)
    codes = jnp.sum(jnp.where(rank[None, :] == index[:, None], code[None, :], 0), axis=1)
    levels = jnp.arange(len(sets) + 1, dtype=jnp.int32)
    ends = jnp.sum((in_set[None, :] < levels[:, None]).astype(jnp.int32), axis=1)
    return codes, ends


class Spread:
    def __init__(self, n_row, n_rep, sections):
        self.n_row, self.n_rep, self.sections = n_row, n_rep, sections
        self.groups = n_row // sections
        self.rep = lax.axis_index("rep")
        row = lax.axis_index("row")
        self.group, self.member = row // sections, row % sections
        self.everyone = [(r, p) for r in range(n_row) for p in range(n_rep)]
        self.halved = n_rep == 2 and self.groups == 2 and sections == 8
        if self.halved:
            self.slots = [(0, 0), (1, 1), (2, 4), (5, 3), (4, 2), (3, 5), (6, 6), (7, 7)]
        else:
            self.slots = [(j, j) for j in range(sections)]

    def flip(self, block, stride):
        return permute(
            block, [((r, p), (r ^ stride, p)) for r, p in self.everyone], self.n_rep
        )

    def flip_either(self, block, even, odd):
        return permute(
            block,
            [((r, p), (r ^ (odd if r & 1 else even), p)) for r, p in self.everyone],
            self.n_rep,
        )

    def swap(self, block):
        return permute(block, [((r, p), (r, 1 - p)) for r, p in self.everyone], self.n_rep)

    def run_halved(self, parts, consume):
        n = self.sections
        across = [
            ((r, p), ((r + n) % self.n_row, r // n)) for r, p in self.everyone if p == r & 1
        ]
        came = [permute(part, across, self.n_rep) for part in parts]
        start = [jnp.where(self.group == self.rep, x, y) for x, y in zip(parts, came)]
        first = [self.flip_either(part, 2, 4) for part in start]
        second = [self.flip_either(part, 4, 2) for part in start]
        near = [self.flip(part, 1) for part in start]
        done = consume([whole(start), whole(near)], None)
        halves = first
        if len(first) == 1:
            half = first[0].shape[0] // 2
            halves = [first[0][:half], first[0][half:]]
        third = [self.flip_either(part, 4, 2) for part in halves]
        near_first = [self.flip(part, 1) for part in first]
        near_second = [self.flip(part, 1) for part in second]
        done = consume([whole(x) for x in (first, near_first, second, near_second)], done)
        third[1], done = lax.optimization_barrier((third[1], done))
        if len(first) == 1:
            third[0], done = lax.optimization_barrier((third[0], done))
        near_third = [self.flip(part, 1) for part in third]
        done = consume([whole(third)], done)
        return consume([whole(near_third)], done)

    def run_whole(self, block, consume):
        start = block
        for d in range(1, self.groups):
            came = permute(
                block,
                [
                    ((p * self.sections + m, p), (((p + d) % self.groups) * self.sections + m, p))
                    for p in range(self.n_rep)
                    for m in range(self.sections)
                ],
                self.n_rep,
            )
            start = jnp.where(self.group == (self.rep + d) % self.groups, came, start)
        blocks = {0: start}
        for b in reversed(range(self.sections.bit_length() - 1)):
            for j in list(blocks):
                blocks[j ^ (1 << b)] = self.flip(blocks[j], 1 << b)
        return consume([whole([blocks[j]]) for j in range(self.sections)], None)


def per_device(
    n_row, n_rep, features, adjacency, tile_live, w_self, w_neigh, bias_vector, pos_pairs, neg_pairs
):
    blocksize = features.shape[0]
    sections = tile_live.shape[1]
    n_pairs = pos_pairs.shape[1]
    share = blocksize // n_rep
    spread = Spread(n_row, n_rep, sections)
    rep, slots = spread.rep, spread.slots

    fetched, added = {}, []

    def add_tiles(blocks, earlier):
        members = slots[len(added) : len(added) + len(blocks)]
        added.extend(members)
        left = slots[len(added) :]
        last = left if 0 < len(left) <= 2 and not fetched else []
        tiles = [fetched[slot] for slot in members] if members[0] in fetched else None
        total, more = aggregate(tile_live, adjacency, blocks, members, earlier, tiles, last)
        fetched.update(zip(last, more))
        return total

    if spread.halved:
        partial = spread.run_halved([features], add_tiles)
    else:
        partial = spread.run_whole(features, add_tiles)

    sets = [slots[:2], slots[2:6], [slots[6]], [slots[7]]] if spread.halved else [slots]
    codes, ends = order_pairs(
        jnp.concatenate([pos_pairs[0], neg_pairs[0]], axis=0), spread.member, sets, blocksize
    )
    def embed(feats, summed):
        projected = jnp.dot(feats, w_self, preferred_element_type=jnp.float32) + bias_vector
        projected = projected + jnp.dot(
            summed.astype(jnp.bfloat16), w_neigh, preferred_element_type=jnp.float32
        )
        scale = lax.rsqrt(jnp.mean(projected * projected, axis=-1, keepdims=True) + 1e-06)
        return (projected * scale).astype(jnp.bfloat16)

    if spread.halved:
        own = []
        for i in range(2):
            rows = slice(i * share, (i + 1) * share)
            other = spread.swap(partial[rows].astype(jnp.bfloat16))
            own.append(embed(features[rows], partial[rows] + other.astype(jnp.float32)))
    else:
        own_feats = lax.dynamic_slice_in_dim(features, rep * share, share, 0)
        embedding = embed(own_feats, lax.psum_scatter(partial, "rep", scatter_dimension=0, tiled=True))

    scored, output = [], []

    def score(queries, blocks, earlier):
        limits = ends
        if len(scored) == 1:
            limits, earlier = lax.optimization_barrier((ends, earlier))
            limits, earlier = lax.optimization_barrier((jnp.maximum(limits, 0), earlier))
        scored.append(len(blocks))
        write_rows = share if spread.halved and len(scored) == 1 else 0
        *rows, pos_loss, neg_loss = score_pairs(
            codes, limits, len(scored) - 1, queries, blocks, n_pairs, earlier, write_rows
        )
        output.extend(rows)
        return pos_loss, neg_loss

    if spread.halved:
        block = jnp.concatenate(own, axis=0)
        losses = spread.run_halved(own, functools.partial(score, block))
        embedding = output[0]
    else:
        block = lax.all_gather(embedding, "rep", axis=0, tiled=True)
        losses = spread.run_whole(block, functools.partial(score, block))
    return (embedding, losses[0][None], losses[1][None])


def solution(mesh):
    return jax.shard_map(
        functools.partial(per_device, mesh.shape["row"], mesh.shape["rep"]),
        mesh=mesh,
        in_specs=(
            P("row", None),
            P("row", "rep"),
            P("row", "rep"),
            P(),
            P(),
            P(),
            P("row", "rep", None),
            P("row", "rep", None),
        ),
        out_specs=(P(("row", "rep"), None), P("row", "rep", None), P("row", "rep", None)),
        check_vma=False,
    )
```
